32 devices in a mesh: feat: 8 (over z, y), cls: 4 (over x, core).
Axes of the slice: x: 2, y: 2, z: 4, core: 2. Of those that a mesh axis runs over, the one named last changes fastest.
Arguments:
- inputs: bfloat16 [2, 1024, 360], P(None, 'feat'), may hold values from -6 to 6
- projection: bfloat16 [360, 65536], P(None, 'feat'), may hold values from -0.3125 to 0.3125
- offsets: int32 [65536], P('feat'), may hold values from 0 to 65520
- labels: int32 [2, 1024], replicated, may hold values from 0 to 4999
- weights: float32 [65536, 5000], P('feat', 'cls'), may hold values from -6 to 6
Outputs:
- updated_weights: float32 [65536, 5000], P('feat', 'cls')
- losses: float32 [2], replicated
The draws below stay inside these ranges and needn't reach their ends.
All inputs are finite; a program needn't handle non-finite values.
Results may differ from the reference program's by a relative error of at most 0.00061.
Values may be sent and summed in bfloat16 or wider, within the bound.
No kernel may reach another device: no remote copies, remote signals or barrier semaphores. Data moves between devices by JAX's collectives and lax.ppermute only.
A program may use at most 192 MiB of HBM per device.

```python
import math
import jax
import jax.numpy as jnp
from jax import lax

DIN = 360
NFEAT = 65536
NCLS = 5000
FRAMES = 1024
PANELS = 2


def place_ends(result, key, low, high):
    place = [jax.random.randint(jax.random.fold_in(key, axis), (), 0, length) for axis, length in enumerate(result.shape)]
    main_axis = result.shape.index(max(result.shape))
    next_to = place[:main_axis] + [(place[main_axis] + 1) % result.shape[main_axis]] + place[main_axis + 1:]
    return result.at[tuple(place)].set(low).at[tuple(next_to)].set(high)


def levels(stream_key, dims, shards, smallest, largest):
    gain = 1.0
    for dim, shards_of in shards:
        draws = jax.random.uniform(jax.random.fold_in(jax.random.fold_in(stream_key, 6), dim), (shards_of,), jnp.float32, smallest / len(shards), largest / len(shards))
        gain = gain * jnp.repeat(jnp.exp(draws), dims[dim] // shards_of).reshape((-1,) + (1,) * (len(dims) - 1 - dim))
    return gain


def centred(stream_key, extent, scale, reach, pieces=(), kind=jnp.bfloat16):
    level = levels(stream_key, extent, pieces, -0.22, 0.18) if pieces else 1.0
    array = jax.random.normal(stream_key, extent, jnp.float32) * scale * level
    return jnp.minimum(jnp.maximum(array, -reach), reach).astype(kind)


def setup_inputs(seed: int = 0) -> dict:
    keys = jax.random.split(jax.random.key(seed), 6)
    inputs = centred(keys[0], (PANELS, FRAMES, DIN), 1.0, 6.0, ((1, 8),))
    projection = centred(keys[1], (DIN, NFEAT), DIN ** -0.5, 0.3125, ((1, 8),))
    offsets = place_ends(jax.random.randint(keys[2], (NFEAT,), 0, 65521), jax.random.fold_in(keys[2], 1), 0, 65520).astype(jnp.int32)
    labels = place_ends(jax.random.randint(keys[3], (PANELS, FRAMES), 0, NCLS), jax.random.fold_in(keys[3], 1), 0, NCLS - 1).astype(jnp.int32)
    weights = centred(keys[4], (NFEAT, NCLS), 1.0, 6.0, ((0, 8), (1, 4)), jnp.float32)
    return {"inputs": inputs, "projection": projection, "offsets": offsets, "labels": labels, "weights": weights}


learning_rate = 10.0

def reference(inputs, projection, offsets, labels, weights):
    phase = offsets.astype(jnp.float32) * (2.0 * math.pi / 65521.0) - math.pi
    block = math.gcd(NFEAT, 4096)
    blocks = NFEAT // block
    classes = jnp.arange(NCLS, dtype=jnp.int32)
    feature_scale = math.sqrt(2.0 / NFEAT)
    losses = []
    for panel_index in range(PANELS):
        features = (feature_scale * jnp.cos(jnp.dot(inputs[panel_index], projection, preferred_element_type=jnp.float32) + phase)).astype(jnp.bfloat16)

        def add_block(running, index):
            start = (index * block).astype(jnp.int32)
            feature_block = lax.dynamic_slice_in_dim(features, start, block, 1)
            weight_block = lax.dynamic_slice_in_dim(weights, start, block, 0).astype(jnp.bfloat16)
            return (running + jnp.dot(feature_block, weight_block, preferred_element_type=jnp.float32), None)
        scores, _ = lax.scan(add_block, jnp.zeros((FRAMES, NCLS), jnp.float32), jnp.arange(blocks, dtype=jnp.int32))
        is_target = labels[panel_index][:, None] == classes[None, :]
        target = lax.optimization_barrier(jnp.sum(jnp.where(is_target, scores, 0.0), axis=1))
        margin = jnp.where(is_target, 0.0, jnp.maximum(0.0, 1.0 + scores - target[:, None]))
        slope = 2.0 * margin / (NCLS - 1)
        others = lax.optimization_barrier(jnp.sum(slope, axis=1))
        losses.append(jnp.sum(lax.optimization_barrier(jnp.sum(margin * margin, axis=1)) / (NCLS - 1)))
        step_grad = jnp.where(is_target, -others[:, None], slope).astype(jnp.bfloat16)

        def update(index):
            start = (index * block).astype(jnp.int32)
            feature_block = lax.dynamic_slice_in_dim(features, start, block, 1)
            weight_block = lax.dynamic_slice_in_dim(weights, start, block, 0)
            gradient = jnp.dot(feature_block.T, step_grad, preferred_element_type=jnp.float32)
            return weight_block - learning_rate * gradient
        weights = lax.map(update, jnp.arange(blocks, dtype=jnp.int32)).reshape(NFEAT, NCLS)
    return (weights, jnp.stack(losses))
```

```python
import functools
import math

import jax
import jax.numpy as jnp
from jax import lax
from jax.experimental import pallas as pl
from jax.experimental.pallas import tpu as pltpu
from jax.sharding import PartitionSpec as P

f32, bf16 = jnp.float32, jnp.bfloat16
learning_rate = 10.0
VMEM_LIMIT = 60 * 1024 * 1024
S0, S1, S2, S3 = 6.283164044274001, -41.33714236744706, 81.34076877058536, -70.99343220053879
NT = (((1,), (1,)), ((), ()))


def features_of(x, p, turns, scale):
    u = jnp.dot(x, p, preferred_element_type=f32) * (0.5 / math.pi) + turns
    t = jnp.abs(u - jnp.round(u)) - 0.25
    s = t * t
    return (t * (scale * S0 + s * (scale * S1 + s * (scale * S2 + s * (scale * S3))))).astype(bf16)


def first_kernel(fb, steps, scale, extra, *refs):
    where_ref, refs = refs[0], refs[1:]
    blocks, refs = refs[:8], refs[8:]
    p_ref, off_ref, w_ref = refs[:3]
    refs = refs[3:]
    if extra:
        e_ref, refs = refs[0], refs[1:]
    f_ref, send_ref, keep_ref, x_ref, now_ref, acc_ref = refs
    j = pl.program_id(0)
    fi, y = where_ref[0], where_ref[1]
    fr = x_ref.shape[0] // 8

    @pl.when(j == 0)
    def _():
        for k in range(8):
            at = pl.multiple_of((fi ^ k) * fr, fr)
            x_ref[pl.ds(at, fr), :] = blocks[k][...].T

    def features(g, slot):
        rows = pl.ds(g * 256, 256)
        turns = off_ref[...].astype(f32) * (1.0 / 65521.0)
        value = features_of(x_ref[rows, :], p_ref[...], turns, scale)
        f_ref[rows, :] = value
        now_ref[slot, rows, :] = value

    def scores(g, slot, start):
        rows = pl.ds(g * 256, 256)
        w = w_ref[...].astype(bf16)
        if extra:
            w = jnp.concatenate([w, e_ref[...]], axis=0)
        s = lax.dot_general(w, now_ref[slot, rows, :], NT, preferred_element_type=f32)
        if start is None:
            acc_ref[g] = s
        else:
            acc_ref[g] += s

    @pl.when(j == 0)
    def _():
        for g in range(4):
            features(g, 0)
            acc_ref[g] = jnp.zeros(acc_ref.shape[1:], f32)

    @pl.when((j > 0) & (j < steps))
    def _():
        for g in range(4):
            features(g, lax.rem(j, 2))
            scores(g, lax.rem(j + 1, 2), 0)

    @pl.when(j == steps)
    def _():
        for g in range(4):
            scores(g, (steps + 1) % 2, 0)
            low, high = acc_ref[g, :, :fr], acc_ref[g, :, fr:]
            send_ref[g] = jnp.where(y == 0, high, low).astype(bf16)
            keep_ref[g] = jnp.where(y == 0, low, high)


def first_call(where, blocks, projection, offsets, wt, extra, rows, scale, fb=512):
    din, nf = projection.shape
    fr = blocks[0].shape[1]
    frames, steps = 8 * fr, nf // fb
    total = rows + (extra.shape[0] // 4 if extra is not None else 0)
    now = lambda j, w: (0, jnp.minimum(j, steps - 1))
    last = lambda j, w: (0, jnp.maximum(j - 1, 0))
    in_specs = [pl.BlockSpec((din, fr), lambda j, w: (0, 0))] * 8 + [
        pl.BlockSpec((din, fb), now),
        pl.BlockSpec((1, fb), now),
        pl.BlockSpec((rows, fb), last),
    ]
    operands = [where, *blocks, projection, offsets, wt]
    if extra is not None:
        in_specs.append(pl.BlockSpec((extra.shape[0] // 4, fb), lambda j, w: (w[2], jnp.maximum(j - 1, 0))))
        operands.append(extra)
    return pl.pallas_call(
        functools.partial(first_kernel, fb, steps, scale, extra is not None),
        grid_spec=pltpu.PrefetchScalarGridSpec(
            num_scalar_prefetch=1,
            grid=(steps + 1,),
            in_specs=in_specs,
            out_specs=[
                pl.BlockSpec((frames, fb), now),
                pl.BlockSpec((4, total, fr), lambda j, w: (0, 0, 0)),
                pl.BlockSpec((4, total, fr), lambda j, w: (0, 0, 0)),
            ],
            scratch_shapes=[
                pltpu.VMEM((frames, din), bf16),
                pltpu.VMEM((2, frames, fb), bf16),
                pltpu.VMEM((4, total, 2 * fr), f32),
            ],
        ),
        out_shape=[
            jax.ShapeDtypeStruct((frames, nf), bf16),
            jax.ShapeDtypeStruct((4, total, fr), bf16),
            jax.ShapeDtypeStruct((4, total, fr), f32),
        ],
        compiler_params=pltpu.CompilerParams(vmem_limit_bytes=VMEM_LIMIT),
        cost_estimate=pl.CostEstimate(
            flops=2 * frames * nf * (din + total), bytes_accessed=nf * (4 * rows + 4 * frames), transcendentals=0
        ),
        name="features_scores",
    )(*operands)


def second_kernel(steps, where_ref, f_ref, w_ref, send_ref, keep_ref, acc_ref):
    j = pl.program_id(0)
    y = where_ref[1]
    fr = send_ref.shape[2]

    @pl.when(j == 0)
    def _():
        acc_ref[...] = jnp.zeros(acc_ref.shape, f32)

    w = w_ref[...].astype(bf16)
    for g in range(4):
        acc_ref[g] += lax.dot_general(w, f_ref[g * 256 : g * 256 + 256, :], NT, preferred_element_type=f32)

    @pl.when(j == steps - 1)
    def _():
        for g in range(4):
            low, high = acc_ref[g, :, :fr], acc_ref[g, :, fr:]
            send_ref[g] = jnp.where(y == 0, high, low).astype(bf16)
            keep_ref[g] = jnp.where(y == 0, low, high)


def second_call(where, features, wt, rows, fb=1024):
    frames, nf = features.shape
    fr, steps = frames // 8, nf // fb
    return pl.pallas_call(
        functools.partial(second_kernel, steps),
        grid_spec=pltpu.PrefetchScalarGridSpec(
            num_scalar_prefetch=1,
            grid=(steps,),
            in_specs=[
                pl.BlockSpec((frames, fb), lambda j, w: (0, j)),
                pl.BlockSpec((rows, fb), lambda j, w: (1, j)),
            ],
            out_specs=[pl.BlockSpec((4, rows, fr), lambda j, w: (0, 0, 0))] * 2,
            scratch_shapes=[pltpu.VMEM((4, rows, 2 * fr), f32)],
        ),
        out_shape=[
            jax.ShapeDtypeStruct((4, rows, fr), bf16),
            jax.ShapeDtypeStruct((4, rows, fr), f32),
        ],
        compiler_params=pltpu.CompilerParams(vmem_limit_bytes=VMEM_LIMIT),
        cost_estimate=pl.CostEstimate(
            flops=2 * frames * nf * rows, bytes_accessed=nf * (4 * rows + 2 * frames), transcendentals=0
        ),
        name="scores",
    )(where, features, wt)


def whole(shape):
    return pl.BlockSpec(shape, lambda *a: (0,) * len(shape))


def small_call(kernel, where, operands, outs, name, scratch=()):
    return pl.pallas_call(
        kernel,
        grid_spec=pltpu.PrefetchScalarGridSpec(
            num_scalar_prefetch=1,
            grid=(1,),
            in_specs=[whole(o.shape) for o in operands],
            out_specs=[whole(s) for s, _ in outs],
            scratch_shapes=list(scratch),
        ),
        out_shape=[jax.ShapeDtypeStruct(s, d) for s, d in outs],
        compiler_params=pltpu.CompilerParams(vmem_limit_bytes=VMEM_LIMIT),
        name=name,
    )(where, *operands)


def add_kernel(where_ref, keep_ref, got_ref, own_ref, a_ref, b_ref, c_ref):
    z = where_ref[3]
    own_ref[...] = keep_ref[z] + got_ref[z].astype(f32)
    for k, out in ((1, a_ref), (2, b_ref), (3, c_ref)):
        out[...] = (keep_ref[z ^ k] + got_ref[z ^ k].astype(f32)).astype(bf16)


def scatter_pair(send):
    return lax.ppermute(send, "feat", [(i, i ^ 1) for i in range(8)])


def scatter_line(where, keep, got):
    shape = keep.shape[1:]
    own, *rest = small_call(add_kernel, where, [keep, got], [(shape, f32)] + [(shape, bf16)] * 3, "pair_sum")
    got = [lax.ppermute(r, "feat", [(i, i ^ (2 * k)) for i in range(8)]) for k, r in zip((1, 2, 3), rest)]
    return [own, *got]


def over_cls(x):
    return [x] + [lax.ppermute(x, "cls", [(i, i ^ k) for i in range(4)]) for k in (1, 2, 3)]


def total(parts):
    return (parts[0] + parts[1].astype(f32)) + (parts[2].astype(f32) + parts[3].astype(f32))


def gram_kernel(where_ref, *refs):
    parts, out = refs[:4], refs[4]
    out[...] = total([p[pl.ds(p.shape[0] - out.shape[0], out.shape[0]), :] for p in parts])


def target_kernel(rows, count, steps_of, where_ref, *refs):
    first, second, refs = refs[:4], refs[4:8], refs[8:]
    lab_ref, refs = refs[0], refs[1:]
    if steps_of:
        gram, ga, gb, refs = refs[:4], refs[4:12], refs[12:20], refs[20:]
    s_ref, t_ref, refs = refs[0], refs[1], refs[2:]
    fr = s_ref.shape[1]
    s_ref[0:rows, :] = total([r[0:rows, :] for r in first])
    s_ref[rows : 2 * rows, :] = total([r[...] for r in second])
    if steps_of:
        fi, q = where_ref[0], where_ref[2]
        hi_ref, lo_ref = refs
        quarter = gram[0].shape[0]
        for k in range(4):
            at = pl.ds(pl.multiple_of((q ^ k) * quarter, quarter), quarter)
            value = gram[k][...]
            hi = value.astype(bf16)
            hi_ref[at, :] = hi
            lo_ref[at, :] = (value - hi.astype(f32)).astype(bf16)
        for r, g in ((0, ga), (rows, gb)):
            change = jnp.zeros((rows, fr), f32)
            for k in range(8):
                at = pl.ds(pl.multiple_of((fi ^ k) * fr, fr), fr)
                change += jnp.dot(g[k][...], hi_ref[at, :], preferred_element_type=f32)
                change += jnp.dot(g[k][...], lo_ref[at, :], preferred_element_type=f32)
            s_ref[r : r + rows, :] -= learning_rate * change
    row = lax.broadcasted_iota(jnp.int32, s_ref.shape, 0)
    is_target = (row + where_ref[2] * count == lab_ref[...]) & (row < count)
    t_ref[...] = jnp.sum(jnp.where(is_target, s_ref[...], 0.0), axis=0, keepdims=True)


def margin_kernel(count, classes, where_ref, s_ref, lab_ref, t0, t1, t2, t3, slope_ref, sums_ref):
    target = (t0[...] + t1[...]) + (t2[...] + t3[...])
    row = lax.broadcasted_iota(jnp.int32, s_ref.shape, 0)
    valid = row < count
    is_target = row + where_ref[2] * count == lab_ref[...]
    margin = jnp.where(valid & ~is_target, jnp.maximum(0.0, 1.0 + s_ref[...] - target), 0.0)
    slope = 2.0 * margin / (classes - 1)
    slope_ref[...] = slope
    sums_ref[0:1, :] = jnp.sum(slope, axis=0, keepdims=True)
    sums_ref[1:2, :] = jnp.sum(margin * margin, axis=0, keepdims=True) / (classes - 1)


def grad_kernel(rows, count, where_ref, slope_ref, lab_ref, s0, s1, s2, s3, a_ref, b_ref, loss_ref):
    sums = (s0[...] + s1[...]) + (s2[...] + s3[...])
    row = lax.broadcasted_iota(jnp.int32, slope_ref.shape, 0)
    is_target = (row + where_ref[2] * count == lab_ref[...]) & (row < count)
    value = jnp.where(is_target, -sums[0:1, :], slope_ref[...]).astype(bf16)
    a_ref[...] = value[:rows]
    b_ref[...] = value[rows:]
    loss_ref[...] = sums[1:2, :]


def spread(block):
    line = [block] + [lax.ppermute(block, "feat", [(i, i ^ (2 * k)) for i in range(8)]) for k in (1, 2, 3)]
    out = []
    for b in line:
        out += [b, lax.ppermute(b, "feat", [(i, i ^ 1) for i in range(8)])]
    return out


def update_kernel(parts, where_ref, *refs):
    rows = refs[0].shape[0]
    grads, refs = refs[: 8 * parts], refs[8 * parts :]
    f_ref, w_ref, out_ref, g_ref = refs[0], refs[1], refs[-2], refs[-1]
    fr = grads[0].shape[1]
    fi = where_ref[0]

    @pl.when(pl.program_id(0) == 0)
    def _():
        for part in range(parts):
            for k in range(8):
                at = pl.ds(pl.multiple_of((fi ^ k) * fr, fr), fr)
                g_ref[part * rows : (part + 1) * rows, at] = grads[8 * part + k][...]

    change = jnp.dot(g_ref[...], f_ref[...], preferred_element_type=f32)
    out_ref[...] = w_ref[...] - learning_rate * change[: out_ref.shape[0]]


def update_call(where, grads, features, wt, place, alias, fb=512):
    frames, nf = features.shape
    rows, fr = grads[0].shape
    parts = len(grads) // 8
    block = wt.shape[0] if parts == 2 else rows
    spec = pl.BlockSpec((block, fb), lambda j, w: (place, j))
    return pl.pallas_call(
        functools.partial(update_kernel, parts),
        grid_spec=pltpu.PrefetchScalarGridSpec(
            num_scalar_prefetch=1,
            grid=(nf // fb,),
            in_specs=[whole((rows, fr))] * len(grads) + [pl.BlockSpec((frames, fb), lambda j, w: (0, j)), spec],
            out_specs=spec,
            scratch_shapes=[pltpu.VMEM((parts * rows, frames), bf16)],
        ),
        out_shape=jax.ShapeDtypeStruct(wt.shape, f32),
        input_output_aliases={len(grads) + 2: 0} if alias else {},
        compiler_params=pltpu.CompilerParams(vmem_limit_bytes=VMEM_LIMIT),
        cost_estimate=pl.CostEstimate(
            flops=2 * frames * nf * rows * parts,
            bytes_accessed=nf * (8 * rows * parts + 2 * frames),
            transcendentals=0,
        ),
        name="update",
    )(where, *grads, features, wt)


def per_device(nfeat, ncls, inputs, projection, offsets, labels, weights):
    fi, q = lax.axis_index("feat"), lax.axis_index("cls")
    where = jnp.stack([fi, fi & 1, q, fi >> 1]).astype(jnp.int32)
    scale = math.sqrt(2.0 / nfeat)
    wt = weights.T
    xt = jnp.swapaxes(inputs, 1, 2)
    fr = xt.shape[2]
    count = wt.shape[0]
    rows = -(-count // 256) * 128
    turns = offsets.reshape(1, -1)
    own_labels = lax.dynamic_slice_in_dim(labels, fi * fr, fr, 1)

    x = [
        [xt[p]] + [lax.ppermute(xt[p], "feat", [(i, i ^ k) for i in range(8)]) for k in range(1, 8)] for p in range(2)
    ]

    def step(p, first, second, extra):
        lab = own_labels[p : p + 1]
        shape = (2 * rows, fr)
        scratch = [pltpu.VMEM((8 * fr, fr), bf16)] * 2 if extra else []
        s, t = small_call(
            functools.partial(target_kernel, rows, count, bool(extra)),
            where,
            [*first, *second, lab, *extra],
            [(shape, f32), ((1, fr), f32)],
            "target",
            scratch,
        )
        slope, sums = small_call(
            functools.partial(margin_kernel, count, ncls),
            where,
            [s, lab, *over_cls(t)],
            [(shape, f32), ((2, fr), f32)],
            "margin",
        )
        ga, gb, loss = small_call(
            functools.partial(grad_kernel, rows, count),
            where,
            [slope, lab, *over_cls(sums)],
            [((rows, fr), bf16), ((rows, fr), bf16), ((1, fr), f32)],
            "step_grad",
        )
        return spread(ga), spread(gb), loss

    f1, send1a, keep1a = first_call(where, x[0], projection, turns, wt, None, rows, scale)
    got1a = scatter_pair(send1a)
    send1b, keep1b = second_call(where, f1, wt, rows)
    got1b = scatter_pair(send1b)
    first1 = scatter_line(where, keep1a, got1a)
    second1 = scatter_line(where, keep1b, got1b)
    f2, send2a, keep2a = first_call(where, x[1], projection, turns, wt, f1, rows, scale)
    got2a = scatter_pair(send2a)
    send2b, keep2b = second_call(where, f2, wt, rows)
    got2b = scatter_pair(send2b)
    g1a, g1b, loss1 = step(0, first1, second1, [])
    first2 = scatter_line(where, keep2a, got2a)
    second2 = scatter_line(where, keep2b, got2b)
    (gram,) = small_call(gram_kernel, where, first2, [((8 * fr // 4, fr), f32)], "gram")
    grams = over_cls(gram)
    g2a, g2b, loss2 = step(1, first2, second2, [*grams, *g1a, *g1b])
    w1 = update_call(where, g1a + g1b, f1, wt, 0, False)
    w2 = update_call(where, g2a, f2, w1, 0, True)
    w2 = update_call(where, g2b, f2, w2, 1, True)
    losses = lax.psum(jnp.stack([jnp.sum(loss1), jnp.sum(loss2)]), "feat")
    return w2.T, losses


def plain_device(nfeat, ncls, inputs, projection, offsets, labels, weights):
    phase = offsets.astype(f32) * (2.0 * math.pi / 65521.0) - math.pi
    classes = jnp.arange(weights.shape[1], dtype=jnp.int32) + lax.axis_index("cls") * weights.shape[1]
    losses = []
    for p in range(inputs.shape[0]):
        x = lax.all_gather(inputs[p], "feat", axis=0, tiled=True)
        features = (math.sqrt(2.0 / nfeat) * jnp.cos(jnp.dot(x, projection, preferred_element_type=f32) + phase)).astype(bf16)
        scores = lax.psum(jnp.dot(features, weights.astype(bf16), preferred_element_type=f32), "feat")
        is_target = labels[p][:, None] == classes[None, :]
        target = lax.psum(jnp.sum(jnp.where(is_target, scores, 0.0), axis=1), "cls")
        margin = jnp.where(is_target, 0.0, jnp.maximum(0.0, 1.0 + scores - target[:, None]))
        slope = 2.0 * margin / (ncls - 1)
        others, row_loss = lax.psum((jnp.sum(slope, axis=1), jnp.sum(margin * margin, axis=1) / (ncls - 1)), "cls")
        grad = jnp.where(is_target, -others[:, None], slope).astype(bf16)
        weights = weights - learning_rate * lax.dot_general(features, grad, (((0,), (0,)), ((), ())), preferred_element_type=f32)
        losses.append(jnp.sum(row_loss))
    return weights, jnp.stack(losses)


def solution(mesh):
    kernels = mesh.shape["feat"] == 8 and mesh.shape["cls"] == 4

    def program(inputs, projection, offsets, labels, weights):
        nfeat, ncls = weights.shape
        body = per_device if kernels and inputs.shape[:2] == (2, 1024) else plain_device
        return jax.shard_map(
            functools.partial(body, nfeat, ncls),
            mesh=mesh,
            in_specs=(P(None, "feat", None), P(None, "feat"), P("feat"), P(), P("feat", "cls")),
            out_specs=(P("feat", "cls"), P()),
            check_vma=False,
        )(inputs, projection, offsets, labels, weights)

    return program
```

```python
import functools
import math

import jax
import jax.numpy as jnp
from jax import lax
from jax.experimental import pallas as pl
from jax.experimental.pallas import tpu as pltpu
from jax.sharding import PartitionSpec as P

f32, bf16 = jnp.float32, jnp.bfloat16
learning_rate = 10.0
VMEM_LIMIT = 60 * 1024 * 1024
S0, S1, S2, S3 = 6.283164044274001, -41.33714236744706, 81.34076877058536, -70.99343220053879
NT = (((1,), (1,)), ((), ()))


def features_of(x, p, turns, scale):
    u = jnp.dot(x, p, preferred_element_type=f32) * (0.5 / math.pi) + turns
    t = jnp.abs(u - jnp.round(u)) - 0.25
    s = t * t
    return (t * (scale * S0 + s * (scale * S1 + s * (scale * S2 + s * (scale * S3))))).astype(bf16)


def after_specs(after):
    return [pl.BlockSpec(memory_space=pl.ANY)] * len(after)


def half_kernel(steps, scale, first, extra, count, skip, blocks, *refs):
    where_ref, xs, refs = refs[0], refs[1 : 1 + blocks], refs[1 + blocks :]
    p_ref, off_ref, w_ref, refs = refs[0], refs[1], refs[2], refs[3:]
    if extra:
        e_ref, refs = refs[0], refs[1:]
    if first:
        pair, refs = refs[:2], refs[2:]
    refs = refs[skip:]
    f_ref, send_ref, keep_ref, refs = refs[0], refs[1], refs[2], refs[3:]
    if first:
        narrow_ref, stack_ref, refs = refs[0], refs[1], refs[2:]
    x_ref, now_ref, acc_ref = refs
    j = pl.program_id(0)
    fr = send_ref.shape[2]
    rows = acc_ref.shape[1] - (2 * fr if extra else 0)

    @pl.when(j == 0)
    def _():
        for k in range(4):
            x_ref[k * fr : (k + 1) * fr, :] = (xs[k][...] if blocks == 4 else xs[k // 2][k % 2]).T
        if first:
            for k in range(2):
                stack_ref[k] = pair[k][...]
        acc_ref[...] = jnp.zeros(acc_ref.shape, f32)

    def features(k, slot):
        at = pl.ds(k * fr, fr)
        turns = off_ref[...].astype(f32) * (1.0 / 65521.0)
        value = features_of(x_ref[at, :], p_ref[...], turns, scale)
        f_ref[at, :] = value
        now_ref[slot, at, :] = value

    def scores(k, slot):
        g, part = k // 2, k % 2
        x = now_ref[slot, g * 2 * fr : (g + 1) * 2 * fr, :]
        if first and k == 0:
            narrow_ref[0:count, :] = w_ref[...].astype(bf16)
            narrow_ref[count:, :] = jnp.zeros((rows - count, narrow_ref.shape[1]), bf16)
        w = narrow_ref if first else w_ref
        cut = rows // 32 * 16
        at = slice(0, cut) if part == 0 else slice(cut, rows)
        acc_ref[g, at, :] += lax.dot_general(w[at, :], x, NT, preferred_element_type=f32)
        if extra and part == 1:
            y = where_ref[1]
            low, high = e_ref[:fr, :], e_ref[fr:, :]
            low, high = jnp.where(y == 0, low, high), jnp.where(y == 0, high, low)
            acc_ref[g, rows : rows + fr, :] += lax.dot_general(low, x, NT, preferred_element_type=f32)
            acc_ref[g, rows + fr :, :] += lax.dot_general(high, x, NT, preferred_element_type=f32)

    @pl.when(j == 0)
    def _():
        for k in range(4):
            features(k, 0)

    @pl.when((j > 0) & (j < steps))
    def _():
        for k in range(4):
            features(k, lax.rem(j, 2))
            scores(k, lax.rem(j + 1, 2))

    @pl.when(j == steps)
    def _():
        for k in range(4):
            scores(k, (steps + 1) % 2)
        for g in range(2):
            keep_ref[g] = acc_ref[g, :, :fr]
            send_ref[g] = acc_ref[g, :, fr:].astype(bf16)


def half_call(where, half, xs, projection, turns, w, count, scale, earlier, pair=None, extra=None, after=(), fb=1024):
    din, nf = projection.shape
    fr = xs[0].shape[-1]
    rows, steps = -(-count // 16) * 16, nf // fb
    first = pair is not None
    total_rows = rows + (2 * fr if extra is not None else 0)
    now = lambda j, w: (0, jnp.minimum(j, steps - 1))
    last = lambda j, w: (0, jnp.maximum(j - 1, 0))
    in_specs = [whole(x.shape) for x in xs] + [
        pl.BlockSpec((din, fb), now),
        pl.BlockSpec((1, fb), now),
        pl.BlockSpec((count if first else rows, fb), last),
    ]
    operands = [where, *xs, projection, turns, w]
    if extra is not None:
        in_specs.append(pl.BlockSpec((2 * fr, fb), lambda j, w: (w[3] ^ w[2], jnp.maximum(j - 1, 0))))
        operands.append(extra)
    if first:
        in_specs += [whole(p.shape) for p in pair]
        operands += pair
    unused = [] if earlier is None else [earlier]
    alias = {} if earlier is None else {len(operands): 0}
    unused += after
    in_specs += after_specs(unused)
    operands += unused
    outs = [((8 * fr, nf), bf16), ((2, total_rows, fr), bf16), ((2, total_rows, fr), f32)]
    out_specs = [
        pl.BlockSpec((4 * fr, fb), lambda j, w: (half, jnp.minimum(j, steps - 1))),
        whole((2, total_rows, fr)),
        whole((2, total_rows, fr)),
    ]
    if first:
        outs += [((rows, nf), bf16), ((2, din, fr), bf16)]
        out_specs += [pl.BlockSpec((rows, fb), last), whole((2, din, fr))]
    return pl.pallas_call(
        functools.partial(half_kernel, steps, scale, first, extra is not None, count, len(unused), len(xs)),
        grid_spec=pltpu.PrefetchScalarGridSpec(
            num_scalar_prefetch=1,
            grid=(steps + 1,),
            in_specs=in_specs,
            out_specs=out_specs,
            scratch_shapes=[
                pltpu.VMEM((4 * fr, din), bf16),
                pltpu.VMEM((2, 4 * fr, fb), bf16),
                pltpu.VMEM((2, total_rows, 2 * fr), f32),
            ],
        ),
        out_shape=[jax.ShapeDtypeStruct(s, d) for s, d in outs],
        input_output_aliases=alias,
        compiler_params=pltpu.CompilerParams(vmem_limit_bytes=VMEM_LIMIT),
        cost_estimate=pl.CostEstimate(
            flops=8 * fr * nf * (din + total_rows), bytes_accessed=nf * (2 * rows + 8 * fr), transcendentals=0
        ),
        name="features_scores",
    )(*operands)


def whole(shape):
    return pl.BlockSpec(shape, lambda *a: (0,) * len(shape))


def small_call(kernel, where, operands, outs, name, scratch=(), after=(), carry=()):
    n, m = 1 + len(operands), len(outs)

    def body(*refs):
        rest = refs[n + len(after) + len(carry) :]
        kernel(*refs[:n], *rest[:m], *rest[m + len(carry) :])

    return pl.pallas_call(
        body,
        grid_spec=pltpu.PrefetchScalarGridSpec(
            num_scalar_prefetch=1,
            grid=(1,),
            in_specs=[whole(o.shape) for o in operands] + after_specs([*after, *carry]),
            out_specs=[whole(s) for s, _ in outs] + after_specs(carry),
            scratch_shapes=list(scratch),
        ),
        out_shape=[jax.ShapeDtypeStruct(s, d) for s, d in outs] + [jax.ShapeDtypeStruct(c.shape, c.dtype) for c in carry],
        input_output_aliases={n + len(after) + i: m + i for i in range(len(carry))},
        compiler_params=pltpu.CompilerParams(vmem_limit_bytes=VMEM_LIMIT),
        cost_estimate=pl.CostEstimate(flops=0, bytes_accessed=8_000_000, transcendentals=0),
        name=name,
    )(where, *operands, *after, *carry)


def far_kernel(where_ref, keep_ref, got_ref, a_ref, b_ref):
    for k, out in ((0, a_ref), (1, b_ref)):
        out[...] = (keep_ref[k] + got_ref[k].astype(f32)).astype(bf16)


def near_kernel(where_ref, keep_ref, got_ref, own_ref, a_ref):
    own_ref[...] = keep_ref[0] + got_ref[0].astype(f32)
    a_ref[...] = (keep_ref[1] + got_ref[1].astype(f32)).astype(bf16)


def swap(x, k):
    return lax.ppermute(x, "feat", [(i, i ^ k) for i in range(8)])


def reduce_far(where, keep, got, after=(), carry=()):
    s = keep.shape[1:]
    return small_call(far_kernel, where, [keep, got], [(s, bf16)] * 2, "far_sums", (), after, carry)


def reduce_near(where, keep, got):
    s = keep.shape[1:]
    return small_call(near_kernel, where, [keep, got], [(s, f32), (s, bf16)], "near_sums")


def over_cls(x):
    return [x] + [lax.ppermute(x, "cls", [(i, i ^ k) for i in range(4)]) for k in (1, 2, 3)]


def total(parts):
    return (parts[0] + parts[1].astype(f32)) + (parts[2].astype(f32) + parts[3].astype(f32))


def gram_kernel(where_ref, *refs):
    parts, out = refs[:4], refs[4]
    out[...] = total([p[pl.ds(p.shape[0] - out.shape[0], out.shape[0]), :] for p in parts])


def target_kernel(count, second, where_ref, *refs):
    parts, lab_ref, refs = refs[:4], refs[4], refs[5:]
    if second:
        gram, grads, refs = refs[:4], refs[4:8], refs[8:]
    s_ref, t_ref, refs = refs[0], refs[1], refs[2:]
    rows, fr = s_ref.shape
    s_ref[...] = total([r[0:rows, :] for r in parts])
    if second:
        fi, q = where_ref[0], where_ref[2]
        hi_ref, lo_ref = refs
        quarter = gram[0].shape[0]
        for k in range(4):
            at = pl.ds(pl.multiple_of((q ^ k) * quarter, quarter), quarter)
            value = gram[k][...]
            hi = value.astype(bf16)
            hi_ref[at, :] = hi
            lo_ref[at, :] = (value - hi.astype(f32)).astype(bf16)
        change = jnp.zeros((rows, fr), f32)
        for k in range(8):
            at = pl.ds(pl.multiple_of((fi ^ k) * fr, fr), fr)
            change += jnp.dot(block_of(grads, k), hi_ref[at, :], preferred_element_type=f32)
            change += jnp.dot(block_of(grads, k), lo_ref[at, :], preferred_element_type=f32)
        s_ref[...] -= learning_rate * change
    row = lax.broadcasted_iota(jnp.int32, s_ref.shape, 0)
    is_target = (row + where_ref[2] * count == lab_ref[...]) & (row < count)
    t_ref[...] = jnp.sum(jnp.where(is_target, s_ref[...], 0.0), axis=0, keepdims=True)


def margin_kernel(count, classes, where_ref, s_ref, lab_ref, target_ref, slope_ref, sums_ref):
    row = lax.broadcasted_iota(jnp.int32, s_ref.shape, 0)
    valid = row < count
    is_target = row + where_ref[2] * count == lab_ref[...]
    margin = jnp.where(valid & ~is_target, jnp.maximum(0.0, 1.0 + s_ref[...] - target_ref[...]), 0.0)
    slope = 2.0 * margin / (classes - 1)
    slope_ref[...] = slope
    sums_ref[0:1, :] = jnp.sum(slope, axis=0, keepdims=True)
    sums_ref[1:2, :] = jnp.sum(margin * margin, axis=0, keepdims=True) / (classes - 1)


def grad_kernel(count, where_ref, slope_ref, lab_ref, sums_ref, g_ref):
    row = lax.broadcasted_iota(jnp.int32, slope_ref.shape, 0)
    is_target = (row + where_ref[2] * count == lab_ref[...]) & (row < count)
    value = jnp.where(is_target, -sums_ref[0:1, :], slope_ref[...])
    rest = sums_ref[1:2, :]
    for n in range(3):
        term = rest.astype(bf16).astype(f32)
        value = jnp.where(row == count + n, term, value)
        rest = rest - term
    g_ref[...] = value.astype(bf16)


def stack_kernel(where_ref, a_ref, b_ref, c_ref, out_ref):
    for k, r in enumerate((a_ref, b_ref, c_ref)):
        out_ref[k] = r[...]


def spread(where, block, after, carry=()):
    line = [swap(block, k) for k in (2, 4, 6)]
    pair = swap(block, 1)
    line, *carry = small_call(stack_kernel, where, line, [((3, *block.shape), bf16)], "line", (), after, carry)
    return [block, pair, line, swap(line, 1)], *carry


def block_of(grads, k):
    return grads[k][...] if k < 2 else grads[2 + k % 2][k // 2 - 1]


def update_kernel(count, skip, first, where_ref, *refs):
    grads, refs = refs[:4], refs[4:]
    f_ref, w_ref, refs = refs[0], refs[1], refs[2:]
    if not first:
        refs0, refs = refs[0], refs[1:]
    refs = refs[skip:]
    out_ref, loss_ref, g_ref = refs
    fr = grads[0].shape[1]

    @pl.when(pl.program_id(0) == 0)
    def _():
        losses = jnp.zeros((8, fr), f32)
        place = lax.broadcasted_iota(jnp.int32, losses.shape, 0)
        for k in range(8):
            g = block_of(grads, k)
            g_ref[:, k * fr : (k + 1) * fr] = g
            loss = sum(g[count + n : count + n + 1, :].astype(f32) for n in range(3))
            losses = jnp.where(place == (where_ref[0] ^ k), loss, losses)
        losses = jnp.sum(losses)
        if first:
            loss_ref[...] = jnp.zeros(loss_ref.shape, f32) + losses
        else:
            lane = lax.broadcasted_iota(jnp.int32, loss_ref.shape, 1)
            loss_ref[...] = jnp.where(lane == 0, refs0[...], losses)

    change = jnp.dot(g_ref[...], f_ref[...], preferred_element_type=f32)
    out_ref[...] = w_ref[...] - learning_rate * change[: out_ref.shape[0]]


def update_call(where, grads, features, wt, earlier=None, part=(0, 1), after=(), loss=None, fb=1024):
    frames, nf = features.shape
    rows, fr = grads[0].shape
    count = wt.shape[0]
    steps = nf // fb // part[1]
    begin = part[0] * steps
    spec = pl.BlockSpec((count, fb), lambda j, w: (0, begin + j))
    alias = {}
    if earlier is wt:
        alias = {6: 0}
    elif earlier is not None:
        alias = {7 if loss is None else 8: 0}
        after = [earlier, *after]
    return pl.pallas_call(
        functools.partial(update_kernel, count, len(after), loss is None),
        grid_spec=pltpu.PrefetchScalarGridSpec(
            num_scalar_prefetch=1,
            grid=(steps,),
            in_specs=[whole(g.shape) for g in grads]
            + [pl.BlockSpec((frames, fb), lambda j, w: (0, begin + j)), spec]
            + [whole((1, 2)) for x in [loss] if x is not None]
            + after_specs(after),
            out_specs=[spec, whole((1, 2))],
            scratch_shapes=[pltpu.VMEM((rows, frames), bf16)],
        ),
        out_shape=[jax.ShapeDtypeStruct(wt.shape, f32), jax.ShapeDtypeStruct((1, 2), f32)],
        input_output_aliases=alias,
        compiler_params=pltpu.CompilerParams(vmem_limit_bytes=VMEM_LIMIT),
        cost_estimate=pl.CostEstimate(
            flops=2 * frames * steps * fb * rows, bytes_accessed=steps * fb * (8 * rows + 2 * frames), transcendentals=0
        ),
        name="update",
    )(where, *grads, features, wt, *([] if loss is None else [loss]), *after)


def per_device(nfeat, ncls, inputs, projection, offsets, labels, weights):
    fi, q = lax.axis_index("feat"), lax.axis_index("cls")
    where = jnp.stack([fi, fi & 1, q, fi >> 1]).astype(jnp.int32)
    scale = math.sqrt(2.0 / nfeat)
    wt = weights.T
    xt = jnp.swapaxes(inputs, 1, 2)
    fr = xt.shape[2]
    count = wt.shape[0]
    rows = -(-count // 16) * 16
    turns = offsets.reshape(1, -1)
    own_labels = lax.dynamic_slice_in_dim(labels, fi * fr, fr, 1)

    def step(p, parts, extra, after=(), carry=()):
        lab = own_labels[p : p + 1]
        shape = (rows, fr)
        scratch = [pltpu.VMEM((8 * fr, fr), bf16)] * 2 if extra else []
        s, t, *carry = small_call(
            functools.partial(target_kernel, count, bool(extra)),
            where,
            [*parts, lab, *extra],
            [(shape, f32), ((1, fr), f32)],
            "target",
            scratch,
            after,
            carry,
        )
        slope, sums = small_call(
            functools.partial(margin_kernel, count, ncls),
            where,
            [s, lab, lax.psum(t, "cls")],
            [(shape, f32), ((2, fr), f32)],
            "margin",
        )
        (g,) = small_call(
            functools.partial(grad_kernel, count),
            where,
            [slope, lab, lax.psum(sums, "cls")],
            [(shape, bf16)],
            "step_grad",
        )
        return g, *carry

    x = [xt[0]] + [swap(xt[0], k) for k in range(1, 8)]
    other = swap(xt[1], 1)
    f1, send_f, keep_f, narrow, pair = half_call(
        where, 1, x[4:], projection, turns, wt, count, scale, None, [xt[1], other]
    )
    got_f = swap(send_f, 1)
    pairs = [pair] + [swap(pair, 2 * k) for k in (1, 2, 3)]
    f1, send_n, keep_n = half_call(where, 0, x[:4], projection, turns, narrow, count, scale, f1)
    r2, r3, send_n = reduce_far(where, keep_f, got_f, [keep_n, *pairs], [send_n])
    r2, r3 = swap(r2, 4), swap(r3, 6)
    own, r1 = reduce_near(where, keep_n, swap(send_n, 1))
    r1 = swap(r1, 2)
    f2, send_f, keep_f = half_call(
        where, 1, pairs[2:], projection, turns, narrow, count, scale, None, None, f1, [own]
    )
    g1, send_f = step(0, [own, r1, r2, r3], [], [keep_f], [send_f])
    got_f = swap(send_f, 1)
    f2, send_n, keep_n = half_call(
        where, 0, pairs[:2], projection, turns, narrow, count, scale, f2, None, f1, [g1]
    )
    all1, send_n = spread(where, g1, [keep_n], [send_n])
    r2, r3 = reduce_far(where, keep_f, got_f, [all1[2]])
    r2, r3 = swap(r2, 4), swap(r3, 6)
    own, r1 = reduce_near(where, keep_n, swap(send_n, 1))
    parts = [own, swap(r1, 2), r2, r3]
    (gram,) = small_call(gram_kernel, where, parts, [((2 * fr, fr), f32)], "gram")
    (g2,) = step(1, parts, [*over_cls(gram), *all1])
    w1, loss1 = update_call(where, all1, f1, wt, None, (0, 2), [g2])
    (all2,) = spread(where, g2, [loss1])
    w1, _ = update_call(where, all1, f1, wt, w1, (1, 2), [all2[2]])
    w2, losses = update_call(where, all2, f2, w1, w1, loss=loss1)
    return w2.T, losses.reshape(2)


def plain_device(nfeat, ncls, inputs, projection, offsets, labels, weights):
    phase = offsets.astype(f32) * (2.0 * math.pi / 65521.0) - math.pi
    classes = jnp.arange(weights.shape[1], dtype=jnp.int32) + lax.axis_index("cls") * weights.shape[1]
    losses = []
    for p in range(inputs.shape[0]):
        x = lax.all_gather(inputs[p], "feat", axis=0, tiled=True)
        features = (math.sqrt(2.0 / nfeat) * jnp.cos(jnp.dot(x, projection, preferred_element_type=f32) + phase)).astype(bf16)
        scores = lax.psum(jnp.dot(features, weights.astype(bf16), preferred_element_type=f32), "feat")
        is_target = labels[p][:, None] == classes[None, :]
        target = lax.psum(jnp.sum(jnp.where(is_target, scores, 0.0), axis=1), "cls")
        margin = jnp.where(is_target, 0.0, jnp.maximum(0.0, 1.0 + scores - target[:, None]))
        slope = 2.0 * margin / (ncls - 1)
        others, row_loss = lax.psum((jnp.sum(slope, axis=1), jnp.sum(margin * margin, axis=1) / (ncls - 1)), "cls")
        grad = jnp.where(is_target, -others[:, None], slope).astype(bf16)
        weights = weights - learning_rate * lax.dot_general(features, grad, (((0,), (0,)), ((), ())), preferred_element_type=f32)
        losses.append(jnp.sum(row_loss))
    return weights, jnp.stack(losses)


def solution(mesh):
    kernels = mesh.shape["feat"] == 8 and mesh.shape["cls"] == 4

    def program(inputs, projection, offsets, labels, weights):
        nfeat, ncls = weights.shape
        body = per_device if kernels and inputs.shape[:2] == (2, 1024) else plain_device
        return jax.shard_map(
            functools.partial(body, nfeat, ncls),
            mesh=mesh,
            in_specs=(P(None, "feat", None), P(None, "feat"), P("feat"), P(), P("feat", "cls")),
            out_specs=(P("feat", "cls"), P()),
            check_vma=False,
        )(inputs, projection, offsets, labels, weights)

    return program
```

```python
import functools
import math

import jax
import jax.numpy as jnp
from jax import lax
from jax.experimental import pallas as pl
from jax.experimental.pallas import tpu as pltpu
from jax.sharding import PartitionSpec as P

f32, bf16 = jnp.float32, jnp.bfloat16
learning_rate = 10.0
VMEM_LIMIT = 44 * 1024 * 1024
S0, S1, S2, S3 = 6.283164044274001, -41.33714236744706, 81.34076877058536, -70.99343220053879
NT = (((1,), (1,)), ((), ()))


def features_of(x, p, turns, scale):
    u = jnp.dot(x, p, preferred_element_type=f32) * (0.5 / math.pi) + turns
    t = jnp.abs(u - jnp.round(u)) - 0.25
    s = t * t
    return (t * (scale * S0 + s * (scale * S1 + s * (scale * S2 + s * (scale * S3))))).astype(bf16)


def after_specs(after):
    return [pl.BlockSpec(memory_space=pl.ANY)] * len(after)


def scores_kernel(steps, scale, first, extra, count, skip, given, *refs):
    where_ref, xs, refs = refs[0], refs[1 : 1 + given], refs[1 + given :]
    p_ref, off_ref, w_ref, refs = refs[0], refs[1], refs[2], refs[3:]
    if extra:
        e_ref, refs = refs[0], refs[1:]
    if first:
        pair, refs = refs[:2], refs[2:]
    refs = refs[skip:]
    f_ref, send_ref, keep_ref, refs = refs[0], refs[1], refs[2], refs[3:]
    if first:
        narrow_ref, stack_ref, refs = refs[0], refs[1], refs[2:]
    x_ref, last_ref, acc_ref = refs
    j = pl.program_id(0)
    fr = send_ref.shape[2]
    rows = acc_ref.shape[1] - (2 * fr if extra else 0)
    groups = acc_ref.shape[0]

    @pl.when(j == 0)
    def _():
        for k in range(2 * groups):
            x_ref[k * fr : (k + 1) * fr, :] = (xs[k][...] if given == 2 * groups else xs[k // 2][k % 2]).T
        if first:
            for k in range(2):
                stack_ref[k] = pair[k][...]
        acc_ref[...] = jnp.zeros(acc_ref.shape, f32)

    def features(k):
        at = pl.ds(k * fr, fr)
        turns = off_ref[...].astype(f32) * (1.0 / 65521.0)
        f_ref[at, :] = features_of(x_ref[at, :], p_ref[...], turns, scale)

    def scores(k):
        g, part = k // 2, k % 2
        x = last_ref[g * 2 * fr : (g + 1) * 2 * fr, :]
        if first and k == 0:
            narrow_ref[0:count, :] = w_ref[...].astype(bf16)
            narrow_ref[count:, :] = jnp.zeros((rows - count, narrow_ref.shape[1]), bf16)
        w = narrow_ref if first else w_ref
        cut = (rows + (2 * fr if extra else 0)) // 32 * 16
        at = slice(0, cut) if part == 0 else slice(cut, rows)
        left = w[at, :]
        if extra and part == 1:
            at, left = slice(cut, rows + 2 * fr), jnp.concatenate([left, e_ref[...]], axis=0)
        acc_ref[g, at, :] += lax.dot_general(left, x, NT, preferred_element_type=f32)

    @pl.when(j == 0)
    def _():
        for k in range(2 * groups):
            features(k)

    @pl.when(j == 0)
    def _():
        last_ref[...] = f_ref[...]

    @pl.when((j > 0) & (j < steps))
    def _():
        for k in range(2 * groups):
            scores(k)
            features(k)
        last_ref[...] = f_ref[...]

    @pl.when(j == steps)
    def _():
        for k in range(2 * groups):
            scores(k)
        for g in range(groups):
            if extra:
                low, high = acc_ref[g, rows : rows + fr, :], acc_ref[g, rows + fr :, :]
                acc_ref[g, rows : rows + fr, :] = jnp.where(where_ref[1] == 0, low, high)
                acc_ref[g, rows + fr :, :] = jnp.where(where_ref[1] == 0, high, low)
            keep_ref[g] = acc_ref[g, :, :fr]
            send_ref[g] = acc_ref[g, :, fr:].astype(bf16)


def scores_call(where, groups, at, xs, projection, turns, w, count, scale, earlier, pair=None, extra=None, after=(), fb=1024):
    din, nf = projection.shape
    fr = xs[0].shape[-1]
    rows, steps = -(-count // 16) * 16, nf // fb
    first = pair is not None
    total_rows = rows + (2 * fr if extra is not None else 0)
    now = lambda j, w: (0, jnp.minimum(j, steps - 1))
    last = lambda j, w: (0, jnp.maximum(j - 1, 0))
    in_specs = [whole(x.shape) for x in xs] + [
        pl.BlockSpec((din, fb), now),
        pl.BlockSpec((1, fb), now),
        pl.BlockSpec((count if first else rows, fb), last),
    ]
    operands = [where, *xs, projection, turns, w]
    if extra is not None:
        in_specs.append(pl.BlockSpec((2 * fr, fb), lambda j, w: (3 - (w[3] ^ w[2]), jnp.maximum(j - 1, 0))))
        operands.append(extra)
    if first:
        in_specs += [whole(p.shape) for p in pair]
        operands += pair
    unused = [] if earlier is None else [earlier]
    alias = {} if earlier is None else {len(operands): 0}
    unused += after
    in_specs += after_specs(unused)
    operands += unused
    outs = [((8 * fr, nf), bf16), ((groups, total_rows, fr), bf16), ((groups, total_rows, fr), f32)]
    out_specs = [
        pl.BlockSpec((2 * groups * fr, fb), lambda j, w: (at, jnp.minimum(j, steps - 1))),
        whole((groups, total_rows, fr)),
        whole((groups, total_rows, fr)),
    ]
    if first:
        outs += [((rows, nf), bf16), ((2, din, fr), bf16)]
        out_specs += [pl.BlockSpec((rows, fb), last), whole((2, din, fr))]
    return pl.pallas_call(
        functools.partial(scores_kernel, steps, scale, first, extra is not None, count, len(unused), len(xs)),
        grid_spec=pltpu.PrefetchScalarGridSpec(
            num_scalar_prefetch=1,
            grid=(steps + 1,),
            in_specs=in_specs,
            out_specs=out_specs,
            scratch_shapes=[
                pltpu.VMEM((2 * groups * fr, din), bf16),
                pltpu.VMEM((2 * groups * fr, fb), bf16),
                pltpu.VMEM((groups, total_rows, 2 * fr), f32),
            ],
        ),
        out_shape=[jax.ShapeDtypeStruct(s, d) for s, d in outs],
        input_output_aliases=alias,
        compiler_params=pltpu.CompilerParams(vmem_limit_bytes=VMEM_LIMIT),
        cost_estimate=pl.CostEstimate(
            flops=4 * groups * fr * nf * (din + total_rows), bytes_accessed=nf * (2 * rows + 4 * groups * fr), transcendentals=0
        ),
        name="features_scores",
    )(*operands)


def whole(shape):
    return pl.BlockSpec(shape, lambda *a: (0,) * len(shape))


def small_call(kernel, where, operands, outs, name, scratch=(), after=(), carry=()):
    n, m = 1 + len(operands), len(outs)

    def body(*refs):
        rest = refs[n + len(after) + len(carry) :]
        kernel(*refs[:n], *rest[:m], *rest[m + len(carry) :])

    return pl.pallas_call(
        body,
        grid_spec=pltpu.PrefetchScalarGridSpec(
            num_scalar_prefetch=1,
            grid=(1,),
            in_specs=[whole(o.shape) for o in operands] + after_specs([*after, *carry]),
            out_specs=[whole(s) for s, _ in outs] + after_specs(carry),
            scratch_shapes=list(scratch),
        ),
        out_shape=[jax.ShapeDtypeStruct(s, d) for s, d in outs] + [jax.ShapeDtypeStruct(c.shape, c.dtype) for c in carry],
        input_output_aliases={n + len(after) + i: m + i for i in range(len(carry))},
        compiler_params=pltpu.CompilerParams(vmem_limit_bytes=24 * 1024 * 1024),
        cost_estimate=pl.CostEstimate(flops=0, bytes_accessed=8_000_000, transcendentals=0),
        name=name,
    )(where, *operands, *after, *carry)


def sums_kernel(where_ref, keep_ref, got_ref, *outs):
    for k, out in enumerate(outs):
        out[...] = (keep_ref[k] + got_ref[k].astype(f32)).astype(out.dtype)


def swap(x, k):
    return lax.ppermute(x, "feat", [(i, i ^ k) for i in range(8)])


def pair_sums(where, keep, got, types, after=(), carry=()):
    s = keep.shape[1:]
    return small_call(sums_kernel, where, [keep, got], [(s, t) for t in types], "pair_sums", (), after, carry)


def over_cls(x):
    return [x] + [lax.ppermute(x, "cls", [(i, i ^ k) for i in range(4)]) for k in (1, 2, 3)]


def total(parts):
    parts = [p.astype(f32) for p in parts]
    return functools.reduce(lambda a, b: a + b, parts[1:], parts[0])


def part_rows(ref, at):
    return ref[0, at, :] if len(ref.shape) == 3 else ref[at, :]


def gram_kernel(where_ref, *refs):
    out = refs[-1]
    rows = out.shape[0]
    out[...] = total([part_rows(p, pl.ds(p.shape[-2] - rows, rows)) for p in refs[:-1]]).astype(bf16)


def target_kernel(count, given, second, where_ref, *refs):
    parts, lab_ref, refs = refs[:given], refs[given], refs[given + 1 :]
    if second:
        gram, grads, refs = refs[:4], refs[4:8], refs[8:]
    s_ref, t_ref, refs = refs[0], refs[1], refs[2:]
    rows, fr = s_ref.shape
    s_ref[...] = total([part_rows(r, slice(0, rows)) for r in parts])
    if second:
        fi, q = where_ref[0], where_ref[2]
        gram_ref = refs[0]
        quarter = gram[0].shape[0]
        for k in range(4):
            at = pl.ds(pl.multiple_of((q ^ k) * quarter, quarter), quarter)
            gram_ref[at, :] = gram[k][...]
        change = jnp.zeros((rows, fr), f32)
        for k in range(8):
            at = pl.ds(pl.multiple_of((fi ^ k) * fr, fr), fr)
            change += jnp.dot(block_of(grads, k), gram_ref[at, :], preferred_element_type=f32)
        s_ref[...] -= learning_rate * change
    row = lax.broadcasted_iota(jnp.int32, s_ref.shape, 0)
    is_target = (row + where_ref[2] * count == lab_ref[...]) & (row < count)
    t_ref[...] = jnp.sum(jnp.where(is_target, s_ref[...], 0.0), axis=0, keepdims=True)


def margin_kernel(count, classes, where_ref, s_ref, lab_ref, target_ref, slope_ref, sums_ref):
    row = lax.broadcasted_iota(jnp.int32, s_ref.shape, 0)
    valid = row < count
    is_target = row + where_ref[2] * count == lab_ref[...]
    margin = jnp.where(valid & ~is_target, jnp.maximum(0.0, 1.0 + s_ref[...] - target_ref[...]), 0.0)
    slope = 2.0 * margin / (classes - 1)
    slope_ref[...] = slope
    sums_ref[0:1, :] = jnp.sum(slope, axis=0, keepdims=True)
    sums_ref[1:2, :] = jnp.sum(margin * margin, axis=0, keepdims=True) / (classes - 1)


def grad_kernel(count, where_ref, slope_ref, lab_ref, sums_ref, g_ref):
    row = lax.broadcasted_iota(jnp.int32, slope_ref.shape, 0)
    is_target = (row + where_ref[2] * count == lab_ref[...]) & (row < count)
    value = jnp.where(is_target, -sums_ref[0:1, :], slope_ref[...])
    rest = sums_ref[1:2, :]
    for n in range(3):
        term = rest.astype(bf16).astype(f32)
        value = jnp.where(row == count + n, term, value)
        rest = rest - term
    g_ref[...] = value.astype(bf16)


def stack_kernel(where_ref, a_ref, b_ref, c_ref, out_ref):
    for k, r in enumerate((a_ref, b_ref, c_ref)):
        out_ref[k] = r[...]


def spread(where, block, after, carry=()):
    line = [swap(block, k) for k in (2, 4, 6)]
    pair = swap(block, 1)
    line, *carry = small_call(stack_kernel, where, line, [((3, *block.shape), bf16)], "line", (), after, carry)
    return [block, pair, line, swap(line, 1)], *carry


def block_of(grads, k):
    return grads[k][...] if k < 2 else grads[2 + k % 2][k // 2 - 1]


def update_kernel(count, skip, first, where_ref, *refs):
    grads, refs = refs[:4], refs[4:]
    f_ref, w_ref, refs = refs[0], refs[1], refs[2:]
    if not first:
        refs0, refs = refs[0], refs[1:]
    refs = refs[skip:]
    out_ref, loss_ref, g_ref = refs
    fr = grads[0].shape[1]

    @pl.when(pl.program_id(0) == 0)
    def _():
        losses = jnp.zeros((8, fr), f32)
        place = lax.broadcasted_iota(jnp.int32, losses.shape, 0)
        for k in range(8):
            g = block_of(grads, k)
            at = 6 - k // 2 * 2 + k % 2
            g_ref[:, at * fr : (at + 1) * fr] = g
            loss = sum(g[count + n : count + n + 1, :].astype(f32) for n in range(3))
            losses = jnp.where(place == (where_ref[0] ^ k), loss, losses)
        losses = jnp.sum(losses)
        if first:
            loss_ref[...] = jnp.zeros(loss_ref.shape, f32) + losses
        else:
            lane = lax.broadcasted_iota(jnp.int32, loss_ref.shape, 1)
            loss_ref[...] = jnp.where(lane == 0, refs0[...], losses)

    change = jnp.dot(g_ref[...], f_ref[...], preferred_element_type=f32)
    out_ref[...] = w_ref[...] - learning_rate * change[: out_ref.shape[0]]


def update_call(where, grads, features, wt, earlier=None, part=(0, 1), after=(), loss=None, fb=1024):
    frames, nf = features.shape
    rows, fr = grads[0].shape
    count = wt.shape[0]
    steps = nf // fb // part[1]
    begin = part[0] * steps
    spec = pl.BlockSpec((count, fb), lambda j, w: (0, begin + j))
    alias = {}
    if earlier is wt:
        alias = {6: 0}
    elif earlier is not None:
        alias = {7 if loss is None else 8: 0}
        after = [earlier, *after]
    return pl.pallas_call(
        functools.partial(update_kernel, count, len(after), loss is None),
        grid_spec=pltpu.PrefetchScalarGridSpec(
            num_scalar_prefetch=1,
            grid=(steps,),
            in_specs=[whole(g.shape) for g in grads]
            + [pl.BlockSpec((frames, fb), lambda j, w: (0, begin + j)), spec]
            + [whole((1, 2)) for x in [loss] if x is not None]
            + after_specs(after),
            out_specs=[spec, whole((1, 2))],
            scratch_shapes=[pltpu.VMEM((rows, frames), bf16)],
        ),
        out_shape=[jax.ShapeDtypeStruct(wt.shape, f32), jax.ShapeDtypeStruct((1, 2), f32)],
        input_output_aliases=alias,
        compiler_params=pltpu.CompilerParams(vmem_limit_bytes=VMEM_LIMIT),
        cost_estimate=pl.CostEstimate(
            flops=2 * frames * steps * fb * rows, bytes_accessed=steps * fb * (8 * rows + 2 * frames), transcendentals=0
        ),
        name="update",
    )(where, *grads, features, wt, *([] if loss is None else [loss]), *after)


def per_device(nfeat, ncls, inputs, projection, offsets, labels, weights):
    fi, q = lax.axis_index("feat"), lax.axis_index("cls")
    where = jnp.stack([fi, fi & 1, q, fi >> 1]).astype(jnp.int32)
    scale = math.sqrt(2.0 / nfeat)
    wt = weights.T
    xt = jnp.swapaxes(inputs, 1, 2)
    fr = xt.shape[2]
    count = wt.shape[0]
    rows = -(-count // 16) * 16
    turns = offsets.reshape(1, -1)
    own_labels = lax.dynamic_slice_in_dim(labels, fi * fr, fr, 1)

    def step(p, parts, extra, after=(), carry=()):
        lab = own_labels[p : p + 1]
        shape = (rows, fr)
        scratch = [pltpu.VMEM((8 * fr, fr), bf16)] if extra else []
        s, t, *carry = small_call(
            functools.partial(target_kernel, count, len(parts), bool(extra)),
            where,
            [*parts, lab, *extra],
            [(shape, f32), ((1, fr), f32)],
            "target",
            scratch,
            after,
            carry,
        )
        slope, sums = small_call(
            functools.partial(margin_kernel, count, ncls),
            where,
            [s, lab, lax.psum(t, "cls")],
            [(shape, f32), ((2, fr), f32)],
            "margin",
        )
        (g,) = small_call(
            functools.partial(grad_kernel, count),
            where,
            [slope, lab, lax.psum(sums, "cls")],
            [(shape, bf16)],
            "step_grad",
        )
        return g, *carry

    x = [xt[0]] + [swap(xt[0], k) for k in range(1, 8)]
    other = swap(xt[1], 1)
    f1, send_b, keep_b, narrow, pair = scores_call(
        where, 3, 0, x[6:8] + x[4:6] + x[2:4], projection, turns, wt, count, scale, None, [xt[1], other]
    )
    got_b = swap(send_b, 1)
    pairs = [swap(pair, 2 * k) for k in (3, 2, 1)] + [pair]
    f1, send_o, keep_o = scores_call(where, 1, 3, x[:2], projection, turns, narrow, count, scale, f1)
    *sums, send_o = pair_sums(where, keep_b, got_b, [bf16] * 3, [keep_o, *pairs], [send_o])
    parts = [keep_o, swap(send_o, 1)] + [swap(r, k) for r, k in zip(sums, (6, 4, 2))]
    f2, send_f, keep_f = scores_call(
        where, 2, 0, pairs[:2], projection, turns, narrow, count, scale, None, None, f1, [sums[0]]
    )
    g1, send_f = step(0, parts, [], [keep_f], [send_f])
    got_f = swap(send_f, 1)
    r3, r2 = pair_sums(where, keep_f, got_f, [bf16] * 2, [g1])
    f2, send_n, keep_n = scores_call(
        where, 2, 1, pairs[2:], projection, turns, narrow, count, scale, f2, None, f1, [r2]
    )
    r3, r2 = swap(r3, 6), swap(r2, 4)
    all1, send_n = spread(where, g1, [keep_n], [send_n])
    r1, own = pair_sums(where, keep_n, swap(send_n, 1), [bf16, f32], [all1[2]])
    parts = [own, swap(r1, 2), r2, r3]
    (gram,) = small_call(gram_kernel, where, parts, [((2 * fr, fr), bf16)], "gram")
    (g2,) = step(1, parts, [*over_cls(gram), *all1])
    w1, loss1 = update_call(where, all1, f1, wt, None, (0, 2), [g2])
    (all2,) = spread(where, g2, [loss1])
    w1, _ = update_call(where, all1, f1, wt, w1, (1, 2), [all2[2]])
    w2, losses = update_call(where, all2, f2, w1, w1, loss=loss1)
    return w2.T, losses.reshape(2)


def plain_device(nfeat, ncls, inputs, projection, offsets, labels, weights):
    phase = offsets.astype(f32) * (2.0 * math.pi / 65521.0) - math.pi
    classes = jnp.arange(weights.shape[1], dtype=jnp.int32) + lax.axis_index("cls") * weights.shape[1]
    losses = []
    for p in range(inputs.shape[0]):
        x = lax.all_gather(inputs[p], "feat", axis=0, tiled=True)
        features = (math.sqrt(2.0 / nfeat) * jnp.cos(jnp.dot(x, projection, preferred_element_type=f32) + phase)).astype(bf16)
        scores = lax.psum(jnp.dot(features, weights.astype(bf16), preferred_element_type=f32), "feat")
        is_target = labels[p][:, None] == classes[None, :]
        target = lax.psum(jnp.sum(jnp.where(is_target, scores, 0.0), axis=1), "cls")
        margin = jnp.where(is_target, 0.0, jnp.maximum(0.0, 1.0 + scores - target[:, None]))
        slope = 2.0 * margin / (ncls - 1)
        others, row_loss = lax.psum((jnp.sum(slope, axis=1), jnp.sum(margin * margin, axis=1) / (ncls - 1)), "cls")
        grad = jnp.where(is_target, -others[:, None], slope).astype(bf16)
        weights = weights - learning_rate * lax.dot_general(features, grad, (((0,), (0,)), ((), ())), preferred_element_type=f32)
        losses.append(jnp.sum(row_loss))
    return weights, jnp.stack(losses)


def solution(mesh):
    kernels = mesh.shape["feat"] == 8 and mesh.shape["cls"] == 4

    def program(inputs, projection, offsets, labels, weights):
        nfeat, ncls = weights.shape
        body = per_device if kernels and inputs.shape[:2] == (2, 1024) else plain_device
        return jax.shard_map(
            functools.partial(body, nfeat, ncls),
            mesh=mesh,
            in_specs=(P(None, "feat", None), P(None, "feat"), P("feat"), P(), P("feat", "cls")),
            out_specs=(P("feat", "cls"), P()),
            check_vma=False,
        )(inputs, projection, offsets, labels, weights)

    return program
```

```python
import functools
import math

import jax
import jax.numpy as jnp
from jax import lax
from jax.experimental import pallas as pl
from jax.experimental.pallas import tpu as pltpu
from jax.sharding import PartitionSpec as P

f32, bf16 = jnp.float32, jnp.bfloat16
learning_rate = 10.0
VMEM_LIMIT = 44 * 1024 * 1024
S0, S1, S2, S3 = 6.283164044274001, -41.33714236744706, 81.34076877058536, -70.99343220053879
NT = (((1,), (1,)), ((), ()))


def features_of(x, p, turns, scale):
    u = jnp.dot(x, p, preferred_element_type=f32) * (0.5 / math.pi) + turns
    t = jnp.abs(u - jnp.round(u)) - 0.25
    s = t * t
    return (t * (scale * S0 + s * (scale * S1 + s * (scale * S2 + s * (scale * S3))))).astype(bf16)


def after_specs(after):
    return [pl.BlockSpec(memory_space=pl.ANY)] * len(after)


def scores_kernel(steps, scale, first, extra, count, skip, given, *refs):
    where_ref, xs, refs = refs[0], refs[1 : 1 + given], refs[1 + given :]
    p_ref, off_ref, w_ref, refs = refs[0], refs[1], refs[2], refs[3:]
    if extra:
        e_ref, refs = refs[0], refs[1:]
    if first:
        pair, refs = refs[:2], refs[2:]
    refs = refs[skip:]
    f_ref, send_ref, keep_ref, refs = refs[0], refs[1], refs[2], refs[3:]
    if first:
        narrow_ref, stack_ref, refs = refs[0], refs[1], refs[2:]
    x_ref, last_ref, acc_ref = refs
    j = pl.program_id(0)
    fr = send_ref.shape[2]
    rows = acc_ref.shape[1] - (2 * fr if extra else 0)
    groups = acc_ref.shape[0]

    @pl.when(j == 0)
    def _():
        for k in range(2 * groups):
            x_ref[k * fr : (k + 1) * fr, :] = (xs[k][...] if given == 2 * groups else xs[k // 2][k % 2]).T
        if first:
            for k in range(2):
                stack_ref[k] = pair[k][...]
        acc_ref[...] = jnp.zeros(acc_ref.shape, f32)

    def features(k):
        at = pl.ds(k * fr, fr)
        turns = off_ref[...].astype(f32) * (1.0 / 65521.0)
        f_ref[at, :] = features_of(x_ref[at, :], p_ref[...], turns, scale)

    def scores(k):
        g, part = k // 2, k % 2
        x = last_ref[g * 2 * fr : (g + 1) * 2 * fr, :]
        if first and k == 0:
            narrow_ref[0:count, :] = w_ref[...].astype(bf16)
            narrow_ref[count:, :] = jnp.zeros((rows - count, narrow_ref.shape[1]), bf16)
        w = narrow_ref if first else w_ref
        cut = (rows + (2 * fr if extra else 0)) // 32 * 16
        at = slice(0, cut) if part == 0 else slice(cut, rows)
        left = w[at, :]
        if extra and part == 1:
            at, left = slice(cut, rows + 2 * fr), jnp.concatenate([left, e_ref[...]], axis=0)
        acc_ref[g, at, :] += lax.dot_general(left, x, NT, preferred_element_type=f32)

    @pl.when(j == 0)
    def _():
        for k in range(2 * groups):
            features(k)

    @pl.when(j == 0)
    def _():
        last_ref[...] = f_ref[...]

    @pl.when((j > 0) & (j < steps))
    def _():
        for k in range(2 * groups):
            scores(k)
            features(k)
        last_ref[...] = f_ref[...]

    @pl.when(j == steps)
    def _():
        for k in range(2 * groups):
            scores(k)
        for g in range(groups):
            if extra:
                low, high = acc_ref[g, rows : rows + fr, :], acc_ref[g, rows + fr :, :]
                acc_ref[g, rows : rows + fr, :] = jnp.where(where_ref[1] == 0, low, high)
                acc_ref[g, rows + fr :, :] = jnp.where(where_ref[1] == 0, high, low)
            keep_ref[g] = acc_ref[g, :, :fr]
            send_ref[g] = acc_ref[g, :, fr:].astype(bf16)


def scores_call(where, groups, at, xs, projection, turns, w, count, scale, earlier, pair=None, extra=None, after=(), fb=1024):
    din, nf = projection.shape
    fr = xs[0].shape[-1]
    rows, steps = -(-count // 16) * 16, nf // fb
    first = pair is not None
    total_rows = rows + (2 * fr if extra is not None else 0)
    now = lambda j, w: (0, jnp.minimum(j, steps - 1))
    last = lambda j, w: (0, jnp.maximum(j - 1, 0))
    in_specs = [whole(x.shape) for x in xs] + [
        pl.BlockSpec((din, fb), now),
        pl.BlockSpec((1, fb), now),
        pl.BlockSpec((count if first else rows, fb), last),
    ]
    operands = [where, *xs, projection, turns, w]
    if extra is not None:
        in_specs.append(pl.BlockSpec((2 * fr, fb), lambda j, w: (3 - (w[3] ^ w[2]), jnp.maximum(j - 1, 0))))
        operands.append(extra)
    if first:
        in_specs += [whole(p.shape) for p in pair]
        operands += pair
    unused = [] if earlier is None else [earlier]
    alias = {} if earlier is None else {len(operands): 0}
    unused += after
    in_specs += after_specs(unused)
    operands += unused
    outs = [((8 * fr, nf), bf16), ((groups, total_rows, fr), bf16), ((groups, total_rows, fr), f32)]
    out_specs = [
        pl.BlockSpec((2 * groups * fr, fb), lambda j, w: (at, jnp.minimum(j, steps - 1))),
        whole((groups, total_rows, fr)),
        whole((groups, total_rows, fr)),
    ]
    if first:
        outs += [((rows, nf), bf16), ((2, din, fr), bf16)]
        out_specs += [pl.BlockSpec((rows, fb), last), whole((2, din, fr))]
    return pl.pallas_call(
        functools.partial(scores_kernel, steps, scale, first, extra is not None, count, len(unused), len(xs)),
        grid_spec=pltpu.PrefetchScalarGridSpec(
            num_scalar_prefetch=1,
            grid=(steps + 1,),
            in_specs=in_specs,
            out_specs=out_specs,
            scratch_shapes=[
                pltpu.VMEM((2 * groups * fr, din), bf16),
                pltpu.VMEM((2 * groups * fr, fb), bf16),
                pltpu.VMEM((groups, total_rows, 2 * fr), f32),
            ],
        ),
        out_shape=[jax.ShapeDtypeStruct(s, d) for s, d in outs],
        input_output_aliases=alias,
        compiler_params=pltpu.CompilerParams(vmem_limit_bytes=VMEM_LIMIT),
        cost_estimate=pl.CostEstimate(
            flops=4 * groups * fr * nf * (din + total_rows), bytes_accessed=nf * (2 * rows + 4 * groups * fr), transcendentals=0
        ),
        name="features_scores",
    )(*operands)


def whole(shape):
    return pl.BlockSpec(shape, lambda *a: (0,) * len(shape))


def small_call(kernel, where, operands, outs, name, scratch=(), after=(), carry=()):
    n, m = 1 + len(operands), len(outs)

    def body(*refs):
        rest = refs[n + len(after) + len(carry) :]
        kernel(*refs[:n], *rest[:m], *rest[m + len(carry) :])

    return pl.pallas_call(
        body,
        grid_spec=pltpu.PrefetchScalarGridSpec(
            num_scalar_prefetch=1,
            grid=(1,),
            in_specs=[whole(o.shape) for o in operands] + after_specs([*after, *carry]),
            out_specs=[whole(s) for s, _ in outs] + after_specs(carry),
            scratch_shapes=list(scratch),
        ),
        out_shape=[jax.ShapeDtypeStruct(s, d) for s, d in outs] + [jax.ShapeDtypeStruct(c.shape, c.dtype) for c in carry],
        input_output_aliases={n + len(after) + i: m + i for i in range(len(carry))},
        compiler_params=pltpu.CompilerParams(vmem_limit_bytes=24 * 1024 * 1024),
        cost_estimate=pl.CostEstimate(flops=0, bytes_accessed=8_000_000, transcendentals=0),
        name=name,
    )(where, *operands, *after, *carry)


def sums_kernel(where_ref, keep_ref, got_ref, *outs):
    for k, out in enumerate(outs):
        out[...] = (keep_ref[k] + got_ref[k].astype(f32)).astype(out.dtype)


def swap(x, k):
    return lax.ppermute(x, "feat", [(i, i ^ k) for i in range(8)])


def pair_sums(where, keep, got, types, after=(), carry=()):
    s = keep.shape[1:]
    return small_call(sums_kernel, where, [keep, got], [(s, t) for t in types], "pair_sums", (), after, carry)


def over_cls(x):
    return [x] + [lax.ppermute(x, "cls", [(i, i ^ k) for i in range(4)]) for k in (1, 2, 3)]


def total(parts):
    parts = [p.astype(f32) for p in parts]
    return functools.reduce(lambda a, b: a + b, parts[1:], parts[0])


def part_rows(ref, at):
    return ref[0, at, :] if len(ref.shape) == 3 else ref[at, :]


def gram_kernel(where_ref, *refs):
    out = refs[-1]
    rows = out.shape[0]
    out[...] = total([part_rows(p, pl.ds(p.shape[-2] - rows, rows)) for p in refs[:-1]]).astype(bf16)


def target_kernel(count, given, second, where_ref, *refs):
    parts, lab_ref, refs = refs[:given], refs[given], refs[given + 1 :]
    if second:
        gram, grads, refs = refs[:4], refs[4:8], refs[8:]
    s_ref, t_ref, refs = refs[0], refs[1], refs[2:]
    rows, fr = s_ref.shape
    s_ref[...] = total([part_rows(r, slice(0, rows)) for r in parts])
    if second:
        fi, q = where_ref[0], where_ref[2]
        gram_ref = refs[0]
        quarter = gram[0].shape[0]
        for k in range(4):
            at = pl.ds(pl.multiple_of((q ^ k) * quarter, quarter), quarter)
            gram_ref[at, :] = gram[k][...]
        change = jnp.zeros((rows, fr), f32)
        for k in range(8):
            at = pl.ds(pl.multiple_of((fi ^ k) * fr, fr), fr)
            change += jnp.dot(block_of(grads, k), gram_ref[at, :], preferred_element_type=f32)
        s_ref[...] -= learning_rate * change
    row = lax.broadcasted_iota(jnp.int32, s_ref.shape, 0)
    is_target = (row + where_ref[2] * count == lab_ref[...]) & (row < count)
    t_ref[...] = jnp.sum(jnp.where(is_target, s_ref[...], 0.0), axis=0, keepdims=True)


def margin_kernel(count, classes, where_ref, s_ref, lab_ref, target_ref, slope_ref, sums_ref):
    row = lax.broadcasted_iota(jnp.int32, s_ref.shape, 0)
    valid = row < count
    is_target = row + where_ref[2] * count == lab_ref[...]
    margin = jnp.where(valid & ~is_target, jnp.maximum(0.0, 1.0 + s_ref[...] - target_ref[...]), 0.0)
    slope = 2.0 * margin / (classes - 1)
    slope_ref[...] = slope
    sums_ref[0:1, :] = jnp.sum(slope, axis=0, keepdims=True)
    sums_ref[1:2, :] = jnp.sum(margin * margin, axis=0, keepdims=True) / (classes - 1)


def grad_kernel(count, where_ref, slope_ref, lab_ref, sums_ref, g_ref):
    row = lax.broadcasted_iota(jnp.int32, slope_ref.shape, 0)
    is_target = (row + where_ref[2] * count == lab_ref[...]) & (row < count)
    value = jnp.where(is_target, -sums_ref[0:1, :], slope_ref[...])
    rest = sums_ref[1:2, :]
    for n in range(3):
        term = rest.astype(bf16).astype(f32)
        value = jnp.where(row == count + n, term, value)
        rest = rest - term
    g_ref[...] = value.astype(bf16)


def stack_kernel(where_ref, a_ref, b_ref, c_ref, out_ref):
    for k, r in enumerate((a_ref, b_ref, c_ref)):
        out_ref[k] = r[...]


def spread(where, block, after, carry=()):
    line = [swap(block, k) for k in (2, 4, 6)]
    pair = swap(block, 1)
    line, *carry = small_call(stack_kernel, where, line, [((3, *block.shape), bf16)], "line", (), [*after, pair], carry)
    return [block, pair, line, swap(line, 1)], *carry


def block_of(grads, k):
    return grads[k][...] if k < 2 else grads[2 + k % 2][k // 2 - 1]


def update_kernel(count, skip, first, where_ref, *refs):
    grads, refs = refs[:4], refs[4:]
    f_ref, w_ref, refs = refs[0], refs[1], refs[2:]
    if not first:
        refs0, refs = refs[0], refs[1:]
    refs = refs[skip:]
    out_ref, loss_ref, g_ref = refs
    fr = grads[0].shape[1]

    @pl.when(pl.program_id(0) == 0)
    def _():
        losses = jnp.zeros((8, fr), f32)
        place = lax.broadcasted_iota(jnp.int32, losses.shape, 0)
        for k in range(8):
            g = block_of(grads, k)
            at = 6 - k // 2 * 2 + k % 2
            g_ref[:, at * fr : (at + 1) * fr] = g
            loss = sum(g[count + n : count + n + 1, :].astype(f32) for n in range(3))
            losses = jnp.where(place == (where_ref[0] ^ k), loss, losses)
        losses = jnp.sum(losses)
        if first:
            loss_ref[...] = jnp.zeros(loss_ref.shape, f32) + losses
        else:
            lane = lax.broadcasted_iota(jnp.int32, loss_ref.shape, 1)
            loss_ref[...] = jnp.where(lane == 0, refs0[...], losses)

    change = jnp.dot(g_ref[...], f_ref[...], preferred_element_type=f32)
    out_ref[...] = w_ref[...] - learning_rate * change[: out_ref.shape[0]]


def update_call(where, grads, features, wt, earlier=None, part=(0, 1), after=(), loss=None, fb=1024):
    frames, nf = features.shape
    rows, fr = grads[0].shape
    count = wt.shape[0]
    steps = nf // fb // part[1]
    begin = part[0] * steps
    spec = pl.BlockSpec((count, fb), lambda j, w: (0, begin + j))
    alias = {}
    if earlier is wt:
        alias = {6: 0}
    elif earlier is not None:
        alias = {7 if loss is None else 8: 0}
        after = [earlier, *after]
    return pl.pallas_call(
        functools.partial(update_kernel, count, len(after), loss is None),
        grid_spec=pltpu.PrefetchScalarGridSpec(
            num_scalar_prefetch=1,
            grid=(steps,),
            in_specs=[whole(g.shape) for g in grads]
            + [pl.BlockSpec((frames, fb), lambda j, w: (0, begin + j)), spec]
            + [whole((1, 2)) for x in [loss] if x is not None]
            + after_specs(after),
            out_specs=[spec, whole((1, 2))],
            scratch_shapes=[pltpu.VMEM((rows, frames), bf16)],
        ),
        out_shape=[jax.ShapeDtypeStruct(wt.shape, f32), jax.ShapeDtypeStruct((1, 2), f32)],
        input_output_aliases=alias,
        compiler_params=pltpu.CompilerParams(vmem_limit_bytes=VMEM_LIMIT),
        cost_estimate=pl.CostEstimate(
            flops=2 * frames * steps * fb * rows, bytes_accessed=steps * fb * (8 * rows + 2 * frames), transcendentals=0
        ),
        name="update",
    )(where, *grads, features, wt, *([] if loss is None else [loss]), *after)


def per_device(nfeat, ncls, inputs, projection, offsets, labels, weights):
    fi, q = lax.axis_index("feat"), lax.axis_index("cls")
    where = jnp.stack([fi, fi & 1, q, fi >> 1]).astype(jnp.int32)
    scale = math.sqrt(2.0 / nfeat)
    wt = weights.T
    xt = jnp.swapaxes(inputs, 1, 2)
    fr = xt.shape[2]
    count = wt.shape[0]
    rows = -(-count // 16) * 16
    turns = offsets.reshape(1, -1)
    own_labels = lax.dynamic_slice_in_dim(labels, fi * fr, fr, 1)

    def step(p, parts, extra, after=(), carry=()):
        lab = own_labels[p : p + 1]
        shape = (rows, fr)
        scratch = [pltpu.VMEM((8 * fr, fr), bf16)] if extra else []
        s, t, *carry = small_call(
            functools.partial(target_kernel, count, len(parts), bool(extra)),
            where,
            [*parts, lab, *extra],
            [(shape, f32), ((1, fr), f32)],
            "target",
            scratch,
            after,
            carry,
        )
        slope, sums = small_call(
            functools.partial(margin_kernel, count, ncls),
            where,
            [s, lab, lax.psum(t, "cls")],
            [(shape, f32), ((2, fr), f32)],
            "margin",
        )
        (g,) = small_call(
            functools.partial(grad_kernel, count),
            where,
            [slope, lab, lax.psum(sums, "cls")],
            [(shape, bf16)],
            "step_grad",
        )
        return g, *carry

    x = [xt[0]] + [swap(xt[0], k) for k in range(1, 8)]
    other = swap(xt[1], 1)
    f1, send_b, keep_b, narrow, pair = scores_call(
        where, 3, 0, x[6:8] + x[4:6] + x[2:4], projection, turns, wt, count, scale, None, [xt[1], other]
    )
    got_b = swap(send_b, 1)
    pairs = [swap(pair, 2 * k) for k in (3, 2, 1)] + [pair]
    f1, send_o, keep_o = scores_call(where, 1, 3, x[:2], projection, turns, narrow, count, scale, f1)
    *sums, send_o = pair_sums(where, keep_b, got_b, [bf16] * 3, [keep_o, *pairs], [send_o])
    parts = [keep_o, swap(send_o, 1)] + [swap(r, k) for r, k in zip(sums, (6, 4, 2))]
    f2, send_f, keep_f = scores_call(
        where, 2, 0, pairs[:2], projection, turns, narrow, count, scale, None, None, f1, [sums[0]]
    )
    g1, send_f = step(0, parts, [], [keep_f], [send_f])
    got_f = swap(send_f, 1)
    r3, r2 = pair_sums(where, keep_f, got_f, [bf16] * 2, [g1])
    f2, send_n, keep_n = scores_call(
        where, 2, 1, pairs[2:], projection, turns, narrow, count, scale, f2, None, f1, [r2]
    )
    r3, r2 = swap(r3, 6), swap(r2, 4)
    all1, send_n = spread(where, g1, [keep_n], [send_n])
    r1, own = pair_sums(where, keep_n, swap(send_n, 1), [bf16, f32], [all1[2]])
    parts = [own, swap(r1, 2), r2, r3]
    (gram,) = small_call(gram_kernel, where, parts, [((2 * fr, fr), bf16)], "gram")
    (g2,) = step(1, parts, [*over_cls(gram), *all1])
    w1, loss1 = update_call(where, all1, f1, wt, None, (0, 2), [g2])
    (all2,) = spread(where, g2, [loss1])
    w1, _ = update_call(where, all1, f1, wt, w1, (1, 2), [all2[2]])
    w2, losses = update_call(where, all2, f2, w1, w1, loss=loss1)
    return w2.T, losses.reshape(2)


def plain_device(nfeat, ncls, inputs, projection, offsets, labels, weights):
    phase = offsets.astype(f32) * (2.0 * math.pi / 65521.0) - math.pi
    classes = jnp.arange(weights.shape[1], dtype=jnp.int32) + lax.axis_index("cls") * weights.shape[1]
    losses = []
    for p in range(inputs.shape[0]):
        x = lax.all_gather(inputs[p], "feat", axis=0, tiled=True)
        features = (math.sqrt(2.0 / nfeat) * jnp.cos(jnp.dot(x, projection, preferred_element_type=f32) + phase)).astype(bf16)
        scores = lax.psum(jnp.dot(features, weights.astype(bf16), preferred_element_type=f32), "feat")
        is_target = labels[p][:, None] == classes[None, :]
        target = lax.psum(jnp.sum(jnp.where(is_target, scores, 0.0), axis=1), "cls")
        margin = jnp.where(is_target, 0.0, jnp.maximum(0.0, 1.0 + scores - target[:, None]))
        slope = 2.0 * margin / (ncls - 1)
        others, row_loss = lax.psum((jnp.sum(slope, axis=1), jnp.sum(margin * margin, axis=1) / (ncls - 1)), "cls")
        grad = jnp.where(is_target, -others[:, None], slope).astype(bf16)
        weights = weights - learning_rate * lax.dot_general(features, grad, (((0,), (0,)), ((), ())), preferred_element_type=f32)
        losses.append(jnp.sum(row_loss))
    return weights, jnp.stack(losses)


def solution(mesh):
    kernels = mesh.shape["feat"] == 8 and mesh.shape["cls"] == 4

    def program(inputs, projection, offsets, labels, weights):
        nfeat, ncls = weights.shape
        body = per_device if kernels and inputs.shape[:2] == (2, 1024) else plain_device
        return jax.shard_map(
            functools.partial(body, nfeat, ncls),
            mesh=mesh,
            in_specs=(P(None, "feat", None), P(None, "feat"), P("feat"), P(), P("feat", "cls")),
            out_specs=(P("feat", "cls"), P()),
            check_vma=False,
        )(inputs, projection, offsets, labels, weights)

    return program
```
